32 devices in a mesh: db: 8 (over z, core), pb: 4 (over y, x).
Axes of the slice: x: 2, y: 2, z: 4, core: 2. Of those that a mesh axis runs over, the one named last changes fastest.
Arguments:
- queries: bfloat16 [128, 768], P('pb', 'db'), may hold values from -6 to 6
- codebook: float32 [192, 16, 4], P('pb'), may hold values from -0.21875 to 0.21875
- codes: int32 [16384, 192], P('db'), may hold values from 0 to 15
- full_rows: bfloat16 [8192, 768], P('db'), may hold values from -0.21875 to 0.21875
- candidates: int32 [128, 256], P('pb'), may hold values from 0 to 8191, as said below
- location: int32 [8192], replicated, may hold values from 0 to 8191, as said below
Outputs:
- approx_scores: bfloat16 [128, 16384], P('pb', 'db')
- rescored: float32 [128, 256], P('pb', 'db')
The draws below stay inside these ranges and needn't reach their ends.
Inputs may be any that keep to these rules, and one draw needn't show every extreme that they name: `candidates`: the owner of a candidate is row_of // 1024; among the candidate slots of the 32 queries of one index of pb in the 256 // 8 columns of one index of db, no owner holds more than 256, and one owner holds exactly 256. Each vector id appears once; vector v is row location[v] of full_rows.
All inputs are finite; a program needn't handle non-finite values.
Results may differ from the reference program's by a relative error of at most 0.005.
Values may be sent and summed in bfloat16 or wider, within the bound.
A program may use at most 64 MiB of HBM per device.

```python
import math
import jax
import jax.numpy as jnp
from jax import lax

D = 768
SUBSP = 192
CODES = 16
SUBDIM = 4
QRY_DEV = 32
FULL_DEV = 1024
CAND = 256
NQ = 128
ROWS = 16384
FULL = 8192
CAP = 256
N_DB = 8
N_PB = 4


def shared_layout(key):
    return jax.random.permutation(jax.random.fold_in(key, 101), FULL).astype(jnp.int32)


def draw_location(key, part):
    layout = shared_layout(key)
    return layout


def draw_candidates(key, part):
    layout = shared_layout(key)
    key = jax.random.fold_in(key, 2)
    inverse = jnp.argsort(layout).astype(jnp.int32)
    block_cols = CAND // N_DB
    slot_count = QRY_DEV * block_cols
    block_keys = jax.random.split(key, N_PB * N_DB)

    def one_block(block_key):
        key_order, key_owner, key_row = jax.random.split(block_key, 3)
        order = jax.random.permutation(key_order, slot_count)
        owner_list = jax.random.permutation(key_owner, N_DB).astype(jnp.int32)
        position = jnp.arange(slot_count, dtype=jnp.int32)
        select = jnp.where(position < CAP, 0, 1 + (position - CAP) % (N_DB - 1))
        owner_at = owner_list[select]
        owner_slot = jnp.zeros((slot_count,), jnp.int32).at[order].set(owner_at)
        inside = jax.random.randint(key_row, (slot_count,), 0, FULL_DEV, dtype=jnp.int32)
        return inverse[owner_slot * FULL_DEV + inside]
    blocks = jax.vmap(one_block)(block_keys)
    blocks = blocks.reshape(N_PB, N_DB, QRY_DEV, block_cols)
    return jnp.transpose(blocks, (0, 2, 1, 3)).reshape(NQ, CAND).astype(jnp.int32)


def plant(values, own_key, low, high):
    place = [jax.random.randint(jax.random.fold_in(own_key, axis), (), 0, length) for axis, length in enumerate(values.shape)]
    main_axis = values.shape.index(max(values.shape))
    beside = place[:main_axis] + [(place[main_axis] + 1) % values.shape[main_axis]] + place[main_axis + 1:]
    return values.at[tuple(place)].set(low).at[tuple(beside)].set(high)


def steps_of(own_key, dims, cuts, low, largest):
    level, own = 1.0, jax.random.fold_in(own_key, 6)
    for dim, shards_of in cuts:
        steps = jnp.exp(jax.random.uniform(jax.random.fold_in(own, dim), (shards_of,), jnp.float32, low / len(cuts), largest / len(cuts)))
        level = level * jnp.repeat(steps, dims[dim] // shards_of).reshape([-1 if axis == dim else 1 for axis in range(len(dims))])
    return level


def bell_draw(key, dims, spread, reach, cuts=(), kind=jnp.bfloat16):
    drawn = spread * jax.random.normal(key, dims, jnp.float32)
    if cuts:
        drawn = drawn * steps_of(key, dims, cuts, -0.22, 0.18)
    return jnp.clip(drawn, -reach, reach).astype(kind)


def setup_inputs(seed: int = 0) -> dict:
    key_of = jax.random.split(jax.random.key(seed), 7)
    return {
        "queries": bell_draw(key_of[0], (NQ, D), 1.0, 6.0, ((0, 4), (1, 8))),
        "codebook": bell_draw(key_of[1], (SUBSP, CODES, SUBDIM), D ** -0.5, 0.21875, ((0, 4),), jnp.float32),
        "codes": plant(jax.random.randint(key_of[2], (ROWS, SUBSP), 0, CODES), jax.random.fold_in(key_of[2], 1), 0, CODES - 1).astype(jnp.int32),
        "full_rows": bell_draw(key_of[3], (FULL, D), D ** -0.5, 0.21875, ((0, 8),)),
        "candidates": draw_candidates(jax.random.fold_in(key_of[6], 71), 0),
        "location": draw_location(jax.random.fold_in(key_of[6], 71), 0),
    }


def reference(queries, codebook, codes, full_rows, candidates, location):
    query_parts = queries.astype(jnp.float32).reshape(NQ, SUBSP, SUBDIM)
    table = jnp.einsum("qsj,scj->qsc", query_parts, codebook, precision=lax.Precision.HIGHEST)
    table = table.reshape(NQ, SUBSP * CODES).astype(jnp.bfloat16)
    table_wide = table.astype(jnp.float32)
    block_rows = math.gcd(ROWS, 512)
    code_blocks = codes.reshape(ROWS // block_rows, block_rows, SUBSP)
    levels = jnp.arange(CODES, dtype=jnp.int32)

    def scan_rows(code_block):
        onehot = (code_block[:, :, None] == levels).astype(jnp.float32).reshape(block_rows, SUBSP * CODES)
        return jnp.dot(table_wide, onehot.T, precision=lax.Precision.HIGHEST).astype(jnp.bfloat16)

    pieces = lax.map(scan_rows, code_blocks)
    approx_scores = jnp.moveaxis(pieces, 0, 1).reshape(NQ, ROWS)
    row_of = location[candidates].astype(jnp.int32)
    query_block = math.gcd(NQ, 256)

    def rescore_rows(inputs):
        query_span, row_span = inputs
        gathered = full_rows[row_span].astype(jnp.float32)
        return jnp.einsum("qk,qck->qc", query_span.astype(jnp.float32), gathered, precision=lax.Precision.HIGHEST)

    rescored = lax.map(rescore_rows, (queries.reshape(NQ // query_block, query_block, D), row_of.reshape(NQ // query_block, query_block, CAND)))
    return approx_scores, rescored.reshape(NQ, CAND)
```

```python
import functools

import jax
import jax.numpy as jnp
from jax import lax
from jax.experimental import pallas as pl
from jax.experimental.pallas import tpu as pltpu
from jax.sharding import PartitionSpec as P

LANES = 128
SUBLANES = 8
CHUNK = 256


def pick_lanes(table, index):
    return jnp.take_along_axis(table, index, axis=1, mode="promise_in_bounds")


def dot_last(a, b):
    return lax.dot_general(a, b, (((1,), (1,)), ((), ())), preferred_element_type=jnp.float32)


def kernel(
    n_db, n_pb,
    q_hbm, cb_hbm, codes_hbm, full_hbm, cand_hbm, loc_hbm,
    approx_ref, resc_ref,
    q_slots, cb_slots, codes_v, full_v, cand_v, loc_v, perm_v, flat_v, table_v, dec_v, row_v, sent_v, got_v,
    local_sem, q_send, q_recv, cb_send, cb_recv, s_send, s_recv,
):
    my_db = lax.axis_index("db")
    my_pb = lax.axis_index("pb")
    query_count, part = q_hbm.shape
    code_count, sub_width, sub_part = cb_hbm.shape
    sub_count, rows_dev = codes_hbm.shape
    full_dev, width = full_hbm.shape
    cand_count = cand_hbm.shape[1]
    db_peers = [lax.rem(my_db + step, n_db) for step in range(1, n_db)]
    pb_peers = [lax.rem(my_pb + step, n_pb) for step in range(1, n_pb)]

    def on_device(src, dst, k):
        copy = pltpu.make_async_copy(src, dst, local_sem.at[k])
        copy.start()
        return copy

    barrier = pltpu.get_barrier_semaphore()
    for peer in db_peers:
        pl.semaphore_signal(barrier, inc=1, device_id={"db": peer}, device_id_type=pl.DeviceIdType.MESH)
    for peer in pb_peers:
        pl.semaphore_signal(barrier, inc=1, device_id={"pb": peer}, device_id_type=pl.DeviceIdType.MESH)
    get_loc = on_device(loc_hbm, loc_v, 0)
    get_cand = on_device(cand_hbm, cand_v, 1)
    get_q = on_device(q_hbm, q_slots.at[my_db], 2)
    get_cb = on_device(cb_hbm, cb_slots.at[my_pb], 3)
    get_full = on_device(full_hbm, full_v, 4)
    get_codes = on_device(codes_hbm, codes_v, 5)
    pl.semaphore_wait(barrier, n_db + n_pb - 2)

    def send_queries(peer, slot):
        return pltpu.make_async_remote_copy(
            src_ref=q_hbm, dst_ref=q_slots.at[slot], send_sem=q_send.at[peer], recv_sem=q_recv.at[slot],
            device_id={"db": peer}, device_id_type=pl.DeviceIdType.MESH)

    def send_codebook(peer, slot):
        return pltpu.make_async_remote_copy(
            src_ref=cb_hbm, dst_ref=cb_slots.at[slot], send_sem=cb_send.at[peer], recv_sem=cb_recv.at[slot],
            device_id={"pb": peer}, device_id_type=pl.DeviceIdType.MESH)

    def send_scores(peer, slot):
        return pltpu.make_async_remote_copy(
            src_ref=sent_v.at[peer], dst_ref=got_v.at[slot], send_sem=s_send.at[peer], recv_sem=s_recv.at[slot],
            device_id={"db": peer}, device_id_type=pl.DeviceIdType.MESH)

    for peer in db_peers:
        send_queries(peer, my_db).start()
    for peer in pb_peers:
        send_codebook(peer, my_pb).start()

    halves = cand_count // LANES
    get_loc.wait()
    get_cand.wait()
    ids = [cand_v[:, h * LANES:(h + 1) * LANES] for h in range(halves)]
    highs = [jnp.right_shift(x, 7) for x in ids]
    lows = [jnp.bitwise_and(x, LANES - 1) for x in ids]

    def lookup(step, found):
        block = loc_v[pl.ds(pl.multiple_of(step * SUBLANES, SUBLANES), SUBLANES), :]
        found = list(found)
        for r in range(SUBLANES):
            row = jnp.broadcast_to(block[r:r + 1, :], (query_count, LANES))
            for h in range(halves):
                found[h] = jnp.where(highs[h] == step * SUBLANES + r, pick_lanes(row, lows[h]), found[h])
        return tuple(found)

    zero = jnp.zeros((query_count, LANES), jnp.int32)
    found = lax.fori_loop(0, loc_hbm.shape[0] // SUBLANES, lookup, (zero,) * halves)
    for h in range(halves):
        row_v[:, h * LANES:(h + 1) * LANES] = found[h] - my_db * full_dev

    column = lax.broadcasted_iota(jnp.int32, (1, width), 1)
    member = jnp.zeros((1, width), jnp.int32)
    for j in range(1, sub_width):
        member = member + jnp.where(column >= j * sub_count, 1, 0)
    feature = (column - member * sub_count) * sub_width + member
    perm_v[...] = jnp.where(
        lax.broadcasted_iota(jnp.int32, (width, width), 0) == feature, 1.0, 0.0).astype(jnp.bfloat16)

    get_q.wait()
    for peer in db_peers:
        send_queries(peer, peer).wait_recv()
    queries = jnp.concatenate(
        [q_slots[i].astype(jnp.float32) for i in range(n_db)], axis=1).astype(jnp.bfloat16)
    get_full.wait()
    exact = dot_last(queries, full_v[...])
    picked = []
    for h in range(halves):
        row = row_v[:, h * LANES:(h + 1) * LANES]
        high = jnp.right_shift(row, 7)
        low = jnp.bitwise_and(row, LANES - 1)
        score = jnp.zeros((query_count, LANES), jnp.float32)
        for t in range(full_dev // LANES):
            score = jnp.where(high == t, pick_lanes(exact[:, t * LANES:(t + 1) * LANES], low), score)
        picked.append(score)

    block = cand_count // n_db
    groups = query_count // SUBLANES
    group_of = lax.broadcasted_iota(jnp.int32, (SUBLANES, LANES), 1) // block
    for b in range(n_db):
        half, offset = (b * block) // LANES, (b * block) % LANES
        packed = jnp.zeros((SUBLANES, LANES), jnp.float32)
        for g in range(groups):
            piece = picked[half][g * SUBLANES:(g + 1) * SUBLANES, :]
            shift = (g * block - offset) % LANES
            if shift:
                piece = pltpu.roll(piece, shift, 1)
            packed = jnp.where(group_of == g, piece, packed)
        sent_v[b] = packed
    for peer in db_peers:
        send_scores(peer, my_db).start()

    permuted = jnp.dot(queries, perm_v[...], preferred_element_type=jnp.float32).astype(jnp.bfloat16)
    get_cb.wait()
    for peer in pb_peers:
        send_codebook(peer, peer).wait_recv()
    used = code_count * sub_width
    eye = jnp.where(
        lax.broadcasted_iota(jnp.int32, (sub_part, sub_part), 0)
        == lax.broadcasted_iota(jnp.int32, (sub_part, sub_part), 1), 1.0, 0.0).astype(jnp.bfloat16)
    for i in range(n_pb):
        for c in range(code_count):
            flat_v[i, c * sub_width:(c + 1) * sub_width, :] = cb_slots[i, c]
        flat_v[i, used:, :] = jnp.zeros((LANES - used, sub_part), jnp.float32)
        table_v[i * sub_part:(i + 1) * sub_part, :] = dot_last(eye, flat_v[i].astype(jnp.bfloat16))
    get_codes.wait()

    def scan(step, carry):
        for k in range(2):
            start = pl.multiple_of((step * 2 + k) * CHUNK, CHUNK)
            for h in range(CHUNK // LANES):
                code = codes_v[:, pl.ds(start + h * LANES, LANES)] * sub_width
                for j in range(sub_width):
                    dec_v[k, j * sub_count:(j + 1) * sub_count, h * LANES:(h + 1) * LANES] = pick_lanes(
                        table_v[...], code + j).astype(jnp.bfloat16)
            scores = jnp.dot(permuted, dec_v[k], preferred_element_type=jnp.float32)
            approx_ref[:, pl.ds(start, CHUNK)] = scores.astype(approx_ref.dtype)
        return carry

    lax.fori_loop(0, rows_dev // (2 * CHUNK), scan, 0)

    total = sent_v[my_db]
    for peer in db_peers:
        send_scores(peer, peer).wait_recv()
        total = total + got_v[peer]
    for g in range(groups):
        shift = (-g * block) % LANES
        resc_ref[g * SUBLANES:(g + 1) * SUBLANES, :] = (pltpu.roll(total, shift, 1) if shift else total)[:, :block]
    for peer in db_peers:
        send_queries(peer, my_db).wait_send()
        send_scores(peer, my_db).wait_send()
    for peer in pb_peers:
        send_codebook(peer, my_pb).wait_send()


def local(n_db, n_pb, queries, codebook, codes, full_rows, candidates, location):
    codebook_t = jnp.transpose(codebook, (1, 2, 0))
    codes_t = codes.T
    location_rows = location.reshape(-1, LANES)
    query_count, part = queries.shape
    sub_part, code_count, sub_width = codebook.shape
    rows_dev, sub_count = codes.shape
    full_dev, width = full_rows.shape
    cand_count = candidates.shape[1]
    assert query_count * (cand_count // n_db) <= SUBLANES * LANES
    return pl.pallas_call(
        functools.partial(kernel, n_db, n_pb),
        out_shape=(
            jax.ShapeDtypeStruct((query_count, rows_dev), jnp.bfloat16),
            jax.ShapeDtypeStruct((query_count, cand_count // n_db), jnp.float32),
        ),
        in_specs=[pl.BlockSpec(memory_space=pl.ANY)] * 6,
        out_specs=[pl.BlockSpec(memory_space=pltpu.VMEM)] * 2,
        scratch_shapes=[
            pltpu.VMEM((n_db, query_count, part), jnp.bfloat16),
            pltpu.VMEM((n_pb, code_count, sub_width, sub_part), jnp.float32),
            pltpu.VMEM((sub_count, rows_dev), jnp.int32),
            pltpu.VMEM((full_dev, width), jnp.bfloat16),
            pltpu.VMEM((query_count, cand_count), jnp.int32),
            pltpu.VMEM(location_rows.shape, jnp.int32),
            pltpu.VMEM((width, width), jnp.bfloat16),
            pltpu.VMEM((n_pb, LANES, sub_part), jnp.float32),
            pltpu.VMEM((sub_count, LANES), jnp.float32),
            pltpu.VMEM((2, width, CHUNK), jnp.bfloat16),
            pltpu.VMEM((query_count, cand_count), jnp.int32),
            pltpu.VMEM((n_db, SUBLANES, LANES), jnp.float32),
            pltpu.VMEM((n_db, SUBLANES, LANES), jnp.float32),
            pltpu.SemaphoreType.DMA((6,)),
            pltpu.SemaphoreType.DMA((n_db,)),
            pltpu.SemaphoreType.DMA((n_db,)),
            pltpu.SemaphoreType.DMA((n_pb,)),
            pltpu.SemaphoreType.DMA((n_pb,)),
            pltpu.SemaphoreType.DMA((n_db,)),
            pltpu.SemaphoreType.DMA((n_db,)),
        ],
        compiler_params=pltpu.CompilerParams(
            collective_id=0, has_side_effects=True, vmem_limit_bytes=60 * 1024 * 1024),
    )(queries, codebook_t, codes_t, full_rows, candidates, location_rows)


def solution(mesh):
    in_specs = (
        P("pb", "db"),
        P("pb", None, None),
        P("db", None),
        P("db", None),
        P("pb", None),
        P(),
    )
    out_specs = (P("pb", "db"), P("pb", "db"))
    sizes = mesh.shape
    return jax.shard_map(
        functools.partial(local, sizes["db"], sizes["pb"]),
        mesh=mesh, in_specs=in_specs, out_specs=out_specs, check_vma=False)
```

```python
import functools

import jax
import jax.numpy as jnp
from jax import lax
from jax.experimental import pallas as pl
from jax.experimental.pallas import tpu as pltpu
from jax.sharding import PartitionSpec as P

LANES = 128
SUBLANES = 8
CHUNK = 256


def pick_lanes(table, index):
    return jnp.take_along_axis(table, index, axis=1, mode="promise_in_bounds")


def dot_last(a, b):
    return lax.dot_general(a, b, (((1,), (1,)), ((), ())), preferred_element_type=jnp.float32)


def kernel(
    n_db, n_pb,
    q_hbm, cb_hbm, codes_hbm, full_hbm, cand_hbm, loc_hbm,
    approx_ref, resc_ref,
    q_slots, cb_slots, codes_v, full_v, cand_v, loc_v, perm_v, flat_v, table_v, dec_v, row_v, exact_v, sent_v, got_v,
    local_sem, q_send, q_recv, cb_send, cb_recv, s_send, s_recv,
):
    my_db = lax.axis_index("db")
    my_pb = lax.axis_index("pb")
    query_count, part = q_hbm.shape
    code_count, sub_width, sub_part = cb_hbm.shape
    sub_count, rows_dev = codes_hbm.shape
    full_dev, width = full_hbm.shape
    cand_count = cand_hbm.shape[1]
    db_peers = [lax.rem(my_db + step, n_db) for step in range(1, n_db)]
    pb_peers = [lax.rem(my_pb + step, n_pb) for step in range(1, n_pb)]

    def on_device(src, dst, k):
        copy = pltpu.make_async_copy(src, dst, local_sem.at[k])
        copy.start()
        return copy

    barrier = pltpu.get_barrier_semaphore()
    for peer in db_peers:
        pl.semaphore_signal(barrier, inc=1, device_id={"db": peer}, device_id_type=pl.DeviceIdType.MESH)
    for peer in pb_peers:
        pl.semaphore_signal(barrier, inc=1, device_id={"pb": peer}, device_id_type=pl.DeviceIdType.MESH)
    get_loc = on_device(loc_hbm, loc_v, 0)
    get_cand = on_device(cand_hbm, cand_v, 1)
    get_q = on_device(q_hbm, q_slots.at[my_db], 2)
    get_cb = on_device(cb_hbm, cb_slots.at[my_pb], 3)
    get_full = on_device(full_hbm, full_v, 4)
    get_codes = on_device(codes_hbm, codes_v, 5)

    column = lax.broadcasted_iota(jnp.int32, (1, width), 1)
    member = jnp.zeros((1, width), jnp.int32)
    for j in range(1, sub_width):
        member = member + jnp.where(column >= j * sub_count, 1, 0)
    feature = (column - member * sub_count) * sub_width + member
    perm_v[...] = jnp.where(
        lax.broadcasted_iota(jnp.int32, (width, width), 0) == feature, 1.0, 0.0).astype(jnp.bfloat16)

    pl.semaphore_wait(barrier, n_db + n_pb - 2)

    def send_queries(peer, slot):
        return pltpu.make_async_remote_copy(
            src_ref=q_hbm, dst_ref=q_slots.at[slot], send_sem=q_send.at[peer], recv_sem=q_recv.at[slot],
            device_id={"db": peer}, device_id_type=pl.DeviceIdType.MESH)

    def send_codebook(peer, slot):
        return pltpu.make_async_remote_copy(
            src_ref=cb_hbm, dst_ref=cb_slots.at[slot], send_sem=cb_send.at[peer], recv_sem=cb_recv.at[slot],
            device_id={"pb": peer}, device_id_type=pl.DeviceIdType.MESH)

    def send_scores(peer, slot):
        return pltpu.make_async_remote_copy(
            src_ref=sent_v.at[peer], dst_ref=got_v.at[slot], send_sem=s_send.at[peer], recv_sem=s_recv.at[slot],
            device_id={"db": peer}, device_id_type=pl.DeviceIdType.MESH)

    for peer in db_peers:
        send_queries(peer, my_db).start()
    for peer in pb_peers:
        send_codebook(peer, my_pb).start()

    halves = cand_count // LANES
    get_loc.wait()
    get_cand.wait()
    spots = [(g, h) for g in range(query_count // SUBLANES) for h in range(halves)]
    views = [(slice(g * SUBLANES, (g + 1) * SUBLANES), slice(h * LANES, (h + 1) * LANES)) for g, h in spots]
    highs = [jnp.right_shift(cand_v[view], 7) for view in views]
    lows = [jnp.bitwise_and(cand_v[view], LANES - 1) for view in views]

    def lookup(step, found):
        first = step * SUBLANES
        block = loc_v[pl.ds(pl.multiple_of(first, SUBLANES), SUBLANES), :]
        rows = [jnp.broadcast_to(block[r:r + 1, :], (SUBLANES, LANES)) for r in range(SUBLANES)]
        out = []
        for value, high, low in zip(found, highs, lows):
            for r, row in enumerate(rows):
                value = jnp.where(high == first + r, pick_lanes(row, low), value)
            out.append(value)
        return tuple(out)

    zero = jnp.zeros((SUBLANES, LANES), jnp.int32)
    found = lax.fori_loop(0, loc_hbm.shape[0] // SUBLANES, lookup, (zero,) * len(views))
    for view, value in zip(views, found):
        row_v[view] = value - my_db * full_dev

    get_q.wait()
    for peer in db_peers:
        send_queries(peer, peer).wait_recv()
    queries = jnp.concatenate(
        [q_slots[i].astype(jnp.float32) for i in range(n_db)], axis=1).astype(jnp.bfloat16)
    get_full.wait()
    exact_v[...] = dot_last(queries, full_v[...])
    picked = {}
    for (g, h), view in zip(spots, views):
        row = row_v[view]
        high = jnp.right_shift(row, 7)
        low = jnp.bitwise_and(row, LANES - 1)
        score = jnp.zeros((SUBLANES, LANES), jnp.float32)
        for t in range(full_dev // LANES):
            tile = exact_v[view[0], t * LANES:(t + 1) * LANES]
            score = jnp.where(high == t, pick_lanes(tile, low), score)
        picked[g, h] = score

    block = cand_count // n_db
    groups = query_count // SUBLANES
    group_of = lax.broadcasted_iota(jnp.int32, (SUBLANES, LANES), 1) // block
    for b in range(n_db):
        half, offset = (b * block) // LANES, (b * block) % LANES
        packed = jnp.zeros((SUBLANES, LANES), jnp.float32)
        for g in range(groups):
            piece = picked[g, half]
            shift = (g * block - offset) % LANES
            if shift:
                piece = pltpu.roll(piece, shift, 1)
            packed = jnp.where(group_of == g, piece, packed)
        sent_v[b] = packed
    for peer in db_peers:
        send_scores(peer, my_db).start()

    permuted = jnp.dot(queries, perm_v[...], preferred_element_type=jnp.float32).astype(jnp.bfloat16)
    get_cb.wait()
    for peer in pb_peers:
        send_codebook(peer, peer).wait_recv()
    used = code_count * sub_width
    eye = jnp.where(
        lax.broadcasted_iota(jnp.int32, (sub_part, sub_part), 0)
        == lax.broadcasted_iota(jnp.int32, (sub_part, sub_part), 1), 1.0, 0.0).astype(jnp.bfloat16)
    for i in range(n_pb):
        for c in range(code_count):
            flat_v[i, pl.ds(c, sub_width, stride=code_count), :] = cb_slots[i, c]
        flat_v[i, used:, :] = jnp.zeros((LANES - used, sub_part), jnp.float32)
        table_v[0, i * sub_part:(i + 1) * sub_part, :] = dot_last(eye, flat_v[i].astype(jnp.bfloat16))
    for j in range(1, sub_width):
        table_v[j] = pltpu.roll(table_v[0], LANES - j * code_count, 1)
    get_codes.wait()

    def scan(step, carry):
        for k in range(2):
            start = pl.multiple_of((step * 2 + k) * CHUNK, CHUNK)
            for h in range(CHUNK // LANES):
                for s in range(0, sub_count, 2 * SUBLANES):
                    code = codes_v[s:s + 2 * SUBLANES, pl.ds(start + h * LANES, LANES)]
                    for j in range(sub_width):
                        values = pick_lanes(table_v[j, s:s + 2 * SUBLANES, :], code)
                        dec_v[k, j * sub_count + s:j * sub_count + s + 2 * SUBLANES, h * LANES:(h + 1) * LANES] = (
                            values.astype(jnp.bfloat16))
            scores = jnp.dot(permuted, dec_v[k], preferred_element_type=jnp.float32)
            approx_ref[:, pl.ds(start, CHUNK)] = scores.astype(approx_ref.dtype)
        return carry

    lax.fori_loop(0, rows_dev // (2 * CHUNK), scan, 0)

    total = sent_v[my_db]
    for peer in db_peers:
        send_scores(peer, peer).wait_recv()
        total = total + got_v[peer]
    for g in range(groups):
        shift = (-g * block) % LANES
        resc_ref[g * SUBLANES:(g + 1) * SUBLANES, :] = (pltpu.roll(total, shift, 1) if shift else total)[:, :block]
    for peer in db_peers:
        send_queries(peer, my_db).wait_send()
        send_scores(peer, my_db).wait_send()
    for peer in pb_peers:
        send_codebook(peer, my_pb).wait_send()


def write_out(approx_ref, resc_ref, approx_hbm, resc_hbm, sem):
    copies = [
        pltpu.make_async_copy(approx_ref, approx_hbm, sem.at[0]),
        pltpu.make_async_copy(resc_ref, resc_hbm, sem.at[1]),
    ]
    for copy in copies:
        copy.start()
    for copy in copies:
        copy.wait()


def local(n_db, n_pb, queries, codebook, codes, full_rows, candidates, location):
    codebook_t = jnp.transpose(codebook, (1, 2, 0))
    codes_t = codes.T
    location_rows = location.reshape(-1, LANES)
    query_count, part = queries.shape
    sub_part, code_count, sub_width = codebook.shape
    rows_dev, sub_count = codes.shape
    full_dev, width = full_rows.shape
    cand_count = candidates.shape[1]
    assert query_count * (cand_count // n_db) <= SUBLANES * LANES
    approx, resc = pl.pallas_call(
        functools.partial(kernel, n_db, n_pb),
        out_shape=(
            pltpu.VMEM((query_count, rows_dev), jnp.bfloat16),
            pltpu.VMEM((query_count, cand_count // n_db), jnp.float32),
        ),
        in_specs=[pl.BlockSpec(memory_space=pltpu.HBM)] * 6,
        out_specs=[pl.BlockSpec(memory_space=pltpu.VMEM)] * 2,
        scratch_shapes=[
            pltpu.VMEM((n_db, query_count, part), jnp.bfloat16),
            pltpu.VMEM((n_pb, code_count, sub_width, sub_part), jnp.float32),
            pltpu.VMEM((sub_count, rows_dev), jnp.int32),
            pltpu.VMEM((full_dev, width), jnp.bfloat16),
            pltpu.VMEM((query_count, cand_count), jnp.int32),
            pltpu.VMEM(location_rows.shape, jnp.int32),
            pltpu.VMEM((width, width), jnp.bfloat16),
            pltpu.VMEM((n_pb, LANES, sub_part), jnp.float32),
            pltpu.VMEM((sub_width, sub_count, LANES), jnp.float32),
            pltpu.VMEM((2, width, CHUNK), jnp.bfloat16),
            pltpu.VMEM((query_count, cand_count), jnp.int32),
            pltpu.VMEM((query_count, full_dev), jnp.float32),
            pltpu.VMEM((n_db, SUBLANES, LANES), jnp.float32),
            pltpu.VMEM((n_db, SUBLANES, LANES), jnp.float32),
            pltpu.SemaphoreType.DMA((6,)),
            pltpu.SemaphoreType.DMA((n_db,)),
            pltpu.SemaphoreType.DMA((n_db,)),
            pltpu.SemaphoreType.DMA((n_pb,)),
            pltpu.SemaphoreType.DMA((n_pb,)),
            pltpu.SemaphoreType.DMA((n_db,)),
            pltpu.SemaphoreType.DMA((n_db,)),
        ],
        compiler_params=pltpu.CompilerParams(
            collective_id=0, has_side_effects=True, vmem_limit_bytes=60 * 1024 * 1024),
    )(queries, codebook_t, codes_t, full_rows, candidates, location_rows)
    return pl.pallas_call(
        write_out,
        out_shape=(
            jax.ShapeDtypeStruct((query_count, rows_dev), jnp.bfloat16),
            jax.ShapeDtypeStruct((query_count, cand_count // n_db), jnp.float32),
        ),
        in_specs=[pl.BlockSpec(memory_space=pltpu.VMEM)] * 2,
        out_specs=[pl.BlockSpec(memory_space=pltpu.HBM)] * 2,
        scratch_shapes=[pltpu.SemaphoreType.DMA((2,))],
    )(approx, resc)


def solution(mesh):
    in_specs = (
        P("pb", "db"),
        P("pb", None, None),
        P("db", None),
        P("db", None),
        P("pb", None),
        P(),
    )
    out_specs = (P("pb", "db"), P("pb", "db"))
    sizes = mesh.shape
    return jax.shard_map(
        functools.partial(local, sizes["db"], sizes["pb"]),
        mesh=mesh, in_specs=in_specs, out_specs=out_specs, check_vma=False)
```

```python
import functools

import jax
import jax.numpy as jnp
from jax import lax
from jax.experimental import pallas as pl
from jax.experimental.pallas import tpu as pltpu
from jax.sharding import PartitionSpec as P

LANES = 128
SUBLANES = 8
CHUNK = 256


def pick_lanes(table, index):
    return jnp.take_along_axis(table, index, axis=1, mode="promise_in_bounds")


def dot_last(a, b):
    return lax.dot_general(a, b, (((1,), (1,)), ((), ())), preferred_element_type=jnp.float32)


def kernel(
    n_db, n_pb,
    q_hbm, cb_hbm, codes_hbm, full_hbm, cand_hbm, loc_hbm,
    approx_ref, resc_ref,
    q_slots, cb_slots, codes_v, full_v, cand_v, loc_v, perm_v, flat_v, table_v, dec_v, row_v, exact_v, sent_v, got_v,
    local_sem, q_send, q_recv, cb_send, cb_recv, s_send, s_recv,
):
    my_db = lax.axis_index("db")
    my_pb = lax.axis_index("pb")
    query_count, part = q_hbm.shape
    code_count, sub_width, sub_part = cb_hbm.shape
    sub_count, rows_dev = codes_hbm.shape
    full_dev, width = full_hbm.shape
    cand_count = cand_hbm.shape[1]
    db_peers = [lax.rem(my_db + step, n_db) for step in range(1, n_db)]
    pb_peers = [lax.rem(my_pb + step, n_pb) for step in range(1, n_pb)]

    def on_device(src, dst, k):
        copy = pltpu.make_async_copy(src, dst, local_sem.at[k])
        copy.start()
        return copy

    barrier = pltpu.get_barrier_semaphore()
    for peer in db_peers:
        pl.semaphore_signal(barrier, inc=1, device_id={"db": peer}, device_id_type=pl.DeviceIdType.MESH)
    for peer in pb_peers:
        pl.semaphore_signal(barrier, inc=1, device_id={"pb": peer}, device_id_type=pl.DeviceIdType.MESH)
    get_loc = on_device(loc_hbm, loc_v, 0)
    get_cand = on_device(cand_hbm, cand_v, 1)
    get_q = on_device(q_hbm, q_slots.at[my_db], 2)
    get_cb = on_device(cb_hbm, cb_slots.at[my_pb], 3)
    get_full = on_device(full_hbm, full_v, 4)
    get_codes = on_device(codes_hbm, codes_v, 5)

    column = lax.broadcasted_iota(jnp.int32, (1, width), 1)
    member = jnp.zeros((1, width), jnp.int32)
    for j in range(1, sub_width):
        member = member + jnp.where(column >= j * sub_count, 1, 0)
    feature = (column - member * sub_count) * sub_width + member
    perm_v[...] = jnp.where(
        lax.broadcasted_iota(jnp.int32, (width, width), 0) == feature, 1.0, 0.0).astype(jnp.bfloat16)

    pl.semaphore_wait(barrier, n_db + n_pb - 2)

    def send_queries(peer, slot):
        return pltpu.make_async_remote_copy(
            src_ref=q_hbm, dst_ref=q_slots.at[slot], send_sem=q_send.at[peer], recv_sem=q_recv.at[slot],
            device_id={"db": peer}, device_id_type=pl.DeviceIdType.MESH)

    def send_codebook(peer, slot):
        return pltpu.make_async_remote_copy(
            src_ref=cb_hbm, dst_ref=cb_slots.at[slot], send_sem=cb_send.at[peer], recv_sem=cb_recv.at[slot],
            device_id={"pb": peer}, device_id_type=pl.DeviceIdType.MESH)

    def send_scores(peer, slot):
        return pltpu.make_async_remote_copy(
            src_ref=sent_v.at[peer], dst_ref=got_v.at[slot], send_sem=s_send.at[peer], recv_sem=s_recv.at[slot],
            device_id={"db": peer}, device_id_type=pl.DeviceIdType.MESH)

    for peer in db_peers:
        send_queries(peer, my_db).start()
    for peer in pb_peers:
        send_codebook(peer, my_pb).start()

    halves = cand_count // LANES
    get_loc.wait()
    get_cand.wait()
    spots = [(g, h) for g in range(query_count // SUBLANES) for h in range(halves)]
    views = [(slice(g * SUBLANES, (g + 1) * SUBLANES), slice(h * LANES, (h + 1) * LANES)) for g, h in spots]
    highs = [jnp.right_shift(cand_v[view], 7) for view in views]
    lows = [jnp.bitwise_and(cand_v[view], LANES - 1) for view in views]

    def lookup(step, found):
        first = step * SUBLANES
        block = loc_v[pl.ds(pl.multiple_of(first, SUBLANES), SUBLANES), :]
        rows = [jnp.broadcast_to(block[r:r + 1, :], (SUBLANES, LANES)) for r in range(SUBLANES)]
        out = []
        for value, high, low in zip(found, highs, lows):
            for r, row in enumerate(rows):
                value = jnp.where(high == first + r, pick_lanes(row, low), value)
            out.append(value)
        return tuple(out)

    zero = jnp.zeros((SUBLANES, LANES), jnp.int32)
    found = lax.fori_loop(0, loc_hbm.shape[0] // SUBLANES, lookup, (zero,) * len(views))
    for view, value in zip(views, found):
        row_v[view] = value - my_db * full_dev

    get_q.wait()
    for peer in db_peers:
        send_queries(peer, peer).wait_recv()
    queries = jnp.concatenate(
        [q_slots[i].astype(jnp.float32) for i in range(n_db)], axis=1).astype(jnp.bfloat16)
    get_full.wait()
    exact_v[...] = dot_last(queries, full_v[...])
    picked = {}
    for (g, h), view in zip(spots, views):
        row = row_v[view]
        high = jnp.right_shift(row, 7)
        low = jnp.bitwise_and(row, LANES - 1)
        score = jnp.zeros((SUBLANES, LANES), jnp.float32)
        for t in range(full_dev // LANES):
            tile = exact_v[view[0], t * LANES:(t + 1) * LANES]
            score = jnp.where(high == t, pick_lanes(tile, low), score)
        picked[g, h] = score

    block = cand_count // n_db
    groups = query_count // SUBLANES
    group_of = lax.broadcasted_iota(jnp.int32, (SUBLANES, LANES), 1) // block
    for b in range(n_db):
        half, offset = (b * block) // LANES, (b * block) % LANES
        packed = jnp.zeros((SUBLANES, LANES), jnp.float32)
        for g in range(groups):
            piece = picked[g, half]
            shift = (g * block - offset) % LANES
            if shift:
                piece = pltpu.roll(piece, shift, 1)
            packed = jnp.where(group_of == g, piece, packed)
        sent_v[b] = packed
    for peer in db_peers:
        send_scores(peer, my_db).start()

    permuted = jnp.dot(queries, perm_v[...], preferred_element_type=jnp.float32).astype(jnp.bfloat16)
    get_cb.wait()
    for peer in pb_peers:
        send_codebook(peer, peer).wait_recv()
    used = code_count * sub_width
    eye = jnp.where(
        lax.broadcasted_iota(jnp.int32, (sub_part, sub_part), 0)
        == lax.broadcasted_iota(jnp.int32, (sub_part, sub_part), 1), 1.0, 0.0).astype(jnp.bfloat16)
    for i in range(n_pb):
        for c in range(code_count):
            flat_v[i, pl.ds(c, sub_width, stride=code_count), :] = cb_slots[i, c]
        flat_v[i, used:, :] = jnp.zeros((LANES - used, sub_part), jnp.float32)
        table_v[0, i * sub_part:(i + 1) * sub_part, :] = dot_last(eye, flat_v[i].astype(jnp.bfloat16))
    for j in range(1, sub_width):
        table_v[j] = pltpu.roll(table_v[0], LANES - j * code_count, 1)
    get_codes.wait()

    def scan(step, carry):
        for k in range(2):
            start = pl.multiple_of((step * 2 + k) * CHUNK, CHUNK)
            for h in range(CHUNK // LANES):
                for s in range(0, sub_count, 2 * SUBLANES):
                    code = codes_v[s:s + 2 * SUBLANES, pl.ds(start + h * LANES, LANES)]
                    for j in range(sub_width):
                        values = pick_lanes(table_v[j, s:s + 2 * SUBLANES, :], code)
                        dec_v[k, j * sub_count + s:j * sub_count + s + 2 * SUBLANES, h * LANES:(h + 1) * LANES] = (
                            values.astype(jnp.bfloat16))
            scores = jnp.dot(permuted, dec_v[k], preferred_element_type=jnp.float32)
            approx_ref[:, pl.ds(start, CHUNK)] = scores.astype(approx_ref.dtype)
        return carry

    lax.fori_loop(0, rows_dev // (2 * CHUNK), scan, 0)

    total = sent_v[my_db]
    for peer in db_peers:
        send_scores(peer, peer).wait_recv()
        total = total + got_v[peer]
    for g in range(groups):
        shift = (-g * block) % LANES
        resc_ref[g * SUBLANES:(g + 1) * SUBLANES, :] = (pltpu.roll(total, shift, 1) if shift else total)[:, :block]
    for peer in db_peers:
        send_queries(peer, my_db).wait_send()
        send_scores(peer, my_db).wait_send()
    for peer in pb_peers:
        send_codebook(peer, my_pb).wait_send()


def write_out(approx_ref, resc_ref, approx_hbm, resc_hbm, sem):
    copies = [
        pltpu.make_async_copy(approx_ref, approx_hbm, sem.at[0]),
        pltpu.make_async_copy(resc_ref, resc_hbm, sem.at[1]),
    ]
    for copy in copies:
        copy.start()
    for copy in copies:
        copy.wait()


def local(n_db, n_pb, queries, codebook, codes, full_rows, candidates, location):
    codebook_t = jnp.transpose(codebook, (1, 2, 0))
    codes_t = codes.T
    location_rows = location.reshape(-1, LANES)
    query_count, part = queries.shape
    sub_part, code_count, sub_width = codebook.shape
    rows_dev, sub_count = codes.shape
    full_dev, width = full_rows.shape
    cand_count = candidates.shape[1]
    assert query_count * (cand_count // n_db) <= SUBLANES * LANES
    approx, resc = pl.pallas_call(
        functools.partial(kernel, n_db, n_pb),
        out_shape=(
            pltpu.VMEM((query_count, rows_dev), jnp.bfloat16),
            pltpu.VMEM((query_count, cand_count // n_db), jnp.float32),
        ),
        in_specs=[pl.BlockSpec(memory_space=pltpu.HBM)] * 6,
        out_specs=[pl.BlockSpec(memory_space=pltpu.VMEM)] * 2,
        scratch_shapes=[
            pltpu.VMEM((n_db, query_count, part), jnp.bfloat16),
            pltpu.VMEM((n_pb, code_count, sub_width, sub_part), jnp.float32),
            pltpu.VMEM((sub_count, rows_dev), jnp.int32),
            pltpu.VMEM((full_dev, width), jnp.bfloat16),
            pltpu.VMEM((query_count, cand_count), jnp.int32),
            pltpu.VMEM(location_rows.shape, jnp.int32),
            pltpu.VMEM((width, width), jnp.bfloat16),
            pltpu.VMEM((n_pb, LANES, sub_part), jnp.float32),
            pltpu.VMEM((sub_width, sub_count, LANES), jnp.float32),
            pltpu.VMEM((2, width, CHUNK), jnp.bfloat16),
            pltpu.VMEM((query_count, cand_count), jnp.int32),
            pltpu.VMEM((query_count, full_dev), jnp.float32),
            pltpu.VMEM((n_db, SUBLANES, LANES), jnp.float32),
            pltpu.VMEM((n_db, SUBLANES, LANES), jnp.float32),
            pltpu.SemaphoreType.DMA((6,)),
            pltpu.SemaphoreType.DMA((n_db,)),
            pltpu.SemaphoreType.DMA((n_db,)),
            pltpu.SemaphoreType.DMA((n_pb,)),
            pltpu.SemaphoreType.DMA((n_pb,)),
            pltpu.SemaphoreType.DMA((n_db,)),
            pltpu.SemaphoreType.DMA((n_db,)),
        ],
        compiler_params=pltpu.CompilerParams(
            collective_id=0, has_side_effects=True, vmem_limit_bytes=60 * 1024 * 1024),
    )(queries, codebook_t, codes_t, full_rows, candidates, location_rows)
    return pl.pallas_call(
        write_out,
        out_shape=(
            jax.ShapeDtypeStruct((query_count, rows_dev), jnp.bfloat16),
            jax.ShapeDtypeStruct((query_count, cand_count // n_db), jnp.float32),
        ),
        in_specs=[pl.BlockSpec(memory_space=pltpu.VMEM)] * 2,
        out_specs=[pl.BlockSpec(memory_space=pltpu.HBM)] * 2,
        scratch_shapes=[pltpu.SemaphoreType.DMA((2,))],
        compiler_params=pltpu.CompilerParams(vmem_limit_bytes=1024 * 1024),
    )(approx, resc)


def solution(mesh):
    in_specs = (
        P("pb", "db"),
        P("pb", None, None),
        P("db", None),
        P("db", None),
        P("pb", None),
        P(),
    )
    out_specs = (P("pb", "db"), P("pb", "db"))
    sizes = mesh.shape
    return jax.shard_map(
        functools.partial(local, sizes["db"], sizes["pb"]),
        mesh=mesh, in_specs=in_specs, out_specs=out_specs, check_vma=False)
```
